32 devices in a mesh: span: 4 (over z), xs: 8 (over y, x, core).
Axes of the slice: x: 2, y: 2, z: 4, core: 2. Of those that a mesh axis runs over, the one named last changes fastest.
Arguments:
- source: float32 [64, 32, 2048], P(None, 'span', 'xs'), may hold values from -0.75 to 0.75
- coefficient: float32 [64, 32, 2048], P(None, 'span', 'xs'), may hold values from 2.5 to 5
- volume_matrix: float32 [64, 64], replicated, may hold values from -0.75 to 0.75
- span_lower: float32 [64, 64], replicated, may hold values from -0.375 to 0.375
- span_upper: float32 [64, 64], replicated, may hold values from -0.375 to 0.375
- cross_lower: float32 [64, 64], replicated, may hold values from -0.375 to 0.375
- cross_upper: float32 [64, 64], replicated, may hold values from -0.375 to 0.375
- interface: int32 [4, 8, 128], P('span', 'xs'), may hold values from 0 to 131071
- compliance: float32 [4, 1024, 1024], P('span', 'xs'), may hold values from -0.75 to 0.75
- start_displacement: float32 [4, 8, 128], P('span', 'xs'), may hold values from -8 to 8
Outputs:
- fluid_state: float32 [64, 32, 2048], P(None, 'span', 'xs')
- shell_displacement: float32 [4, 8, 128], P('span', 'xs')
The draws below stay inside these ranges and needn't reach their ends.
All inputs are finite; a program needn't handle non-finite values.
Results may differ from the reference program's by a relative error of at most 0.0001.
Values sent between devices are 32-bit elements; how exact they have to be, the bound alone decides.
A program may use at most 64 MiB of HBM per device.

```python
import jax
import jax.numpy as jnp
from jax import lax

NODES = 64
ES_DEV = 8
EX_DEV = 256
IF_DEV = 128
SUBITERS = 2
KRYLOV = 2
NS = 32
NX = 2048
SPANS = 4
GROUPS = 8
SHELL = 1024
N_SPAN = 4
N_XS = 8


def group_levels(key):
    return jax.random.bernoulli(jax.random.fold_in(key, 7), 0.5, (SPANS, GROUPS))


def draw_coefficient(key, part):
    lowered = group_levels(key)
    spread = jnp.repeat(jnp.repeat(lowered, ES_DEV, axis=0), EX_DEV, axis=1)
    parity = (jnp.arange(NX) % 2).astype(jnp.float32)[None, None, :]
    jitter = 0.3 * jax.random.uniform(jax.random.fold_in(key, 11), (NODES, NS, NX), jnp.float32)
    low_value = 2.5 + 0.6 * parity + jitter
    high_value = 4.1 + 0.6 * (1.0 - parity) + jitter
    return jnp.where(spread[None, :, :], low_value, high_value).astype(jnp.float32)


def draw_start_displacement(key, part):
    lowered = group_levels(key)
    values = 2.0 * jnp.clip(jax.random.normal(jax.random.fold_in(key, 13), (SPANS, GROUPS, IF_DEV), jnp.float32), -3.5, 3.5)
    return jnp.where(lowered[:, :, None], values, 0.0).astype(jnp.float32)


def set_ends(drawn, stream_key, least, top_value):
    longest = drawn.shape.index(max(drawn.shape))
    spots = []
    for shift in (0, 1):
        where = [jax.random.randint(jax.random.fold_in(stream_key, axis), (), 0, length) for axis, length in enumerate(drawn.shape)]
        where[longest] = (where[longest] + shift) % drawn.shape[longest]
        spots.append(tuple(where))
    return drawn.at[spots[0]].set(least).at[spots[1]].set(top_value)


def levels(own_key, extent, cuts, low, largest):
    loudness, own = 1.0, jax.random.fold_in(own_key, 6)
    for dim, parts in cuts:
        draws = jnp.exp(jax.random.uniform(jax.random.fold_in(own, dim), (parts,), jnp.float32, low / len(cuts), largest / len(cuts)))
        loudness = loudness * jnp.repeat(draws, extent[dim] // parts).reshape([-1 if axis == dim else 1 for axis in range(len(extent))])
    return loudness


def centred(key, extent, width, limit, cuts=(), held_as=jnp.bfloat16):
    values = jax.random.normal(key, extent, jnp.float32) * width
    if len(cuts) > 0:
        values = levels(key, extent, cuts, -0.22, 0.18) * values
    return jnp.clip(values, min=-limit, max=limit).astype(held_as)


def setup_inputs(seed: int = 0) -> dict:
    splits = jax.random.split(jax.random.key(seed), 11)
    source = centred(splits[0], (NODES, NS, NX), 0.05, 0.75, ((1, 4), (2, 8)), jnp.float32)
    coefficient = draw_coefficient(jax.random.fold_in(splits[10], 71), 0)
    volume_matrix = centred(splits[2], (NODES, NODES), NODES ** -0.5, 0.75, (), jnp.float32)
    span_lower = centred(splits[3], (NODES, NODES), (4 * NODES) ** -0.5, 0.375, (), jnp.float32)
    span_upper = centred(splits[4], (NODES, NODES), (4 * NODES) ** -0.5, 0.375, (), jnp.float32)
    cross_lower = centred(splits[5], (NODES, NODES), (4 * NODES) ** -0.5, 0.375, (), jnp.float32)
    cross_upper = centred(splits[6], (NODES, NODES), (4 * NODES) ** -0.5, 0.375, (), jnp.float32)
    interface = set_ends(jax.random.randint(splits[7], (SPANS, GROUPS, IF_DEV), 0, NODES * ES_DEV * EX_DEV), jax.random.fold_in(splits[7], 1), 0, (NODES * ES_DEV * EX_DEV) - 1).astype(jnp.int32)
    compliance = centred(splits[8], (SPANS, SHELL, SHELL), (SHELL // 16) ** -0.5, 0.75, ((0, 4), (1, 8)), jnp.float32)
    start_displacement = draw_start_displacement(jax.random.fold_in(splits[10], 71), 0)
    return dict(source=source, coefficient=coefficient, volume_matrix=volume_matrix, span_lower=span_lower, span_upper=span_upper, cross_lower=cross_lower, cross_upper=cross_upper, interface=interface, compliance=compliance, start_displacement=start_displacement)


exact_mode = lax.Precision.HIGHEST

def node_product(matrix, field):
    return jnp.einsum('ab,bsx->asx', matrix, field, precision=exact_mode)

def operate(field, coefficient, mats):
    volume_matrix, span_lower, span_upper, cross_lower, cross_upper = mats
    below = jnp.roll(field, 1, axis=1)
    above = jnp.roll(field, -1, axis=1)
    padded = jnp.pad(field, ((0, 0), (0, 0), (1, 1)))
    left = padded[:, :, :-2]
    right = padded[:, :, 2:]
    result = coefficient * field + node_product(volume_matrix, field)
    result = result - node_product(span_lower, below) - node_product(span_upper, above)
    return result - node_product(cross_lower, left) - node_product(cross_upper, right)

def to_groups(field):
    shaped = field.reshape(NODES, N_SPAN, ES_DEV, N_XS, EX_DEV)
    return shaped.transpose(1, 3, 0, 2, 4).reshape(N_SPAN, N_XS, NODES * ES_DEV * EX_DEV)

def from_groups(blocks):
    shaped = blocks.reshape(N_SPAN, N_XS, NODES, ES_DEV, EX_DEV)
    return shaped.transpose(2, 0, 3, 1, 4).reshape(NODES, N_SPAN * ES_DEV, N_XS * EX_DEV)

def place_one(indices, values):
    return jnp.zeros((NODES * ES_DEV * EX_DEV,), jnp.float32).at[indices].add(values)

def gmres(rhs, coefficient, mats):
    start_norm = jnp.sqrt(jnp.sum(rhs * rhs))
    basis = [rhs / start_norm]
    columns = []
    for step in range(KRYLOV):
        image = operate(basis[-1], coefficient, mats)
        project = jnp.stack([jnp.sum(vector * image) for vector in basis])
        for index in range(step + 1):
            image = image - project[index] * basis[index]
        length = jnp.sqrt(jnp.sum(image * image))
        columns.append(jnp.concatenate([project, length[None], jnp.zeros((KRYLOV - step - 1,), jnp.float32)]))
        basis.append(image / length)
    hessen = jnp.stack(columns, axis=1)
    gram = jnp.dot(hessen.T, hessen, precision=exact_mode)
    target = start_norm * hessen[0]
    factor = jnp.linalg.cholesky(gram)
    coeffs = jax.scipy.linalg.cho_solve((factor, True), target)
    result = coeffs[0] * basis[0]
    for index in range(1, KRYLOV):
        result = result + coeffs[index] * basis[index]
    return result

def reference(source, coefficient, volume_matrix, span_lower, span_upper, cross_lower, cross_upper, interface, compliance, start_displacement):
    mats = (volume_matrix, span_lower, span_upper, cross_lower, cross_upper)
    displacement = start_displacement
    fluid = source
    for sub in range(SUBITERS):
        forcing = jax.vmap(jax.vmap(place_one))(interface, displacement)
        rhs = source + from_groups(forcing)
        fluid = gmres(rhs, coefficient, mats)
        traces = jnp.take_along_axis(to_groups(fluid), interface, axis=2)
        fresh = jnp.einsum('sij,sj->si', compliance, traces.reshape(N_SPAN, N_XS * IF_DEV), precision=exact_mode)
        displacement = 0.5 * fresh.reshape(N_SPAN, N_XS, IF_DEV) + 0.5 * displacement
    return (fluid, displacement)
```

```python
import functools

import jax
import jax.numpy as jnp
from jax import lax
from jax.experimental import pallas as pl
from jax.experimental.pallas import tpu as pltpu
from jax.sharding import PartitionSpec as P

SUBITERS = 2
SHIFT = 3.75
LANES = 128
MESH = pl.DeviceIdType.MESH
f32, bf16 = jnp.float32, jnp.bfloat16


def split(value):
    high = value.astype(bf16)
    return high, (value - high.astype(f32)).astype(bf16)


def mm(a, b):
    return jnp.dot(a, b, preferred_element_type=f32)


def iota(shape, dim):
    return lax.broadcasted_iota(jnp.int32, shape, dim)


def to_column(row):
    k = row.shape[1]
    wide = jnp.broadcast_to(row, (k, k))
    keep = iota((k, k), 0) == iota((k, k), 1)
    return jnp.sum(jnp.where(keep, wide, jnp.zeros_like(wide)), axis=1, keepdims=True)


def to_row(column):
    k = column.shape[0]
    wide = jnp.broadcast_to(column, (k, k))
    keep = iota((k, k), 0) == iota((k, k), 1)
    return jnp.sum(jnp.where(keep, wide, jnp.zeros_like(wide)), axis=0, keepdims=True)


def window(dims, src, coef, vol, slo, sup, clo, cup, face, comp, disp0, out, dout,
           big, side, cs, base, fields, high, low, pick, pick_t, where_x,
           col_out, col_in, part, part_in, total, total_in,
           halo_send, halo_recv, xs_send, xs_recv, sp_send, sp_recv):
    nsp, nxs, N, S, X, K = dims
    sp, xs = lax.axis_index("span"), lax.axis_index("xs")
    barrier = pltpu.get_barrier_semaphore()
    for o in range(1, nxs):
        pl.semaphore_signal(barrier, inc=1, device_id={"xs": lax.rem(xs + o, nxs)}, device_id_type=MESH)
    for o in range(1, nsp):
        pl.semaphore_signal(barrier, inc=1, device_id={"span": lax.rem(sp + o, nsp)}, device_id_type=MESH)

    zero = jnp.zeros((N, N), f32)
    rows = jnp.concatenate([
        jnp.concatenate([-slo[...], vol[...], -sup[...]], axis=1),
        jnp.concatenate([zero, clo[...], zero], axis=1),
        jnp.concatenate([zero, cup[...], zero], axis=1),
    ], axis=0)
    bh, bl = split(rows)
    big[: 3 * N, :] = bh
    big[3 * N :, :] = bl
    for i, m in enumerate((clo, cup)):
        mh, ml = split(m[...])
        side[i, 0] = mh
        side[i, 1] = ml

    index_row = face[...]
    index_col = to_column(index_row.astype(f32)).astype(jnp.int32)

    def row_of(index):
        shift_x, shift_s = X.bit_length() - 1, S.bit_length() - 1
        s = (index >> shift_x) & (S - 1)
        return s * N + (index >> (shift_x + shift_s))

    hot = (iota((S * N, K), 0) == row_of(index_row)).astype(f32).astype(bf16)
    pick[:, :K] = hot
    pick[:, K:] = hot
    pick_t[...] = (iota((K, S * N), 1) == row_of(index_col)).astype(f32).astype(bf16)
    where_x[...] = (iota((K, X), 1) == (index_col & (X - 1))).astype(f32)

    for s in range(S):
        base[s * N : (s + 1) * N, :] = src[:, s, :]
        cs[s * N : (s + 1) * N, :] = coef[:, s, :] - SHIFT

    lane = iota((N, LANES), 1)
    wide = iota((N, X), 1)
    sent = []

    def own(s):
        return slice((s + 1) * N, (s + 2) * N)

    def start_halo(e):
        f, h, l = fields.at[e], high.at[e % 2], low.at[e % 2]
        copies = []

        def send(i, from_ref, to_ref, axis, target):
            c = pltpu.make_async_remote_copy(
                src_ref=from_ref, dst_ref=to_ref, send_sem=halo_send.at[e, i], recv_sem=halo_recv.at[e, i],
                device_id={axis: target}, device_id_type=MESH)
            c.start()
            copies.append(c)
            sent.append(c)

        up, down = lax.rem(sp + 1, nsp), lax.rem(sp + nsp - 1, nsp)
        right, left = lax.rem(xs + 1, nxs), lax.rem(xs + nxs - 1, nxs)
        send(0, f.at[pl.ds(S * N, N)], f.at[pl.ds(0, N)], "span", up)
        send(1, f.at[pl.ds(N, N)], f.at[pl.ds((S + 1) * N, N)], "span", down)
        first = jnp.zeros((N, LANES), f32)
        last = jnp.zeros((N, LANES), f32)
        for s in range(S):
            a = f[own(s), :LANES]
            b = f[own(s), X - LANES :]
            first = jnp.where(lane == s, pltpu.roll(a, s, 1) if s else a, first)
            last = jnp.where(lane == s, pltpu.roll(b, s + 1, 1), last)
        col_out[e, 0] = first
        col_out[e, 1] = last
        send(2, col_out.at[e, 1], col_in.at[e, 0], "xs", right)
        send(3, col_out.at[e, 0], col_in.at[e, 1], "xs", left)
        for s in range(S):
            h[own(s), :], l[own(s), :] = split(f[own(s), :])
        return copies

    def apply(e, target, copies):
        f, h, l = fields.at[e], high.at[e % 2], low.at[e % 2]

        def element_row(s):
            near = slice(s * N, (s + 3) * N)
            xh, xl = h[near, :], l[near, :]
            p = mm(big[...], xh)
            r = p[: 3 * N] + p[3 * N :] + mm(big[: 3 * N, :], xl)
            res = cs[s * N : (s + 1) * N, :] * f[own(s), :] + r[:N]
            res = res - jnp.where(wide == 0, 0.0, pltpu.roll(r[N : 2 * N], 1, 1))
            res = res - jnp.where(wide == X - 1, 0.0, pltpu.roll(r[2 * N :], X - 1, 1))
            target[own(s), :] = res

        for s in range(1, S - 1):
            element_row(s)
        for c in copies:
            c.wait_recv()
        for row in (slice(0, N), slice((S + 1) * N, (S + 2) * N)):
            h[row, :], l[row, :] = split(f[row, :])
        element_row(0)
        element_row(S - 1)
        edges = []
        for i, there in enumerate((xs > 0, xs < nxs - 1)):
            got = jnp.where(there, col_in[e, i], 0.0)
            gh, gl = split(got)
            edges.append(mm(side[i, 0], gh) + mm(side[i, 1], gh) + mm(side[i, 0], gl))
        for s in range(S):
            first = pltpu.roll(edges[0], LANES - s, 1) if s else edges[0]
            target[own(s), :LANES] = target[own(s), :LANES] - jnp.where(lane == 0, first, 0.0)
            last = pltpu.roll(edges[1], LANES - 1 - s, 1)
            target[own(s), X - LANES :] = target[own(s), X - LANES :] - jnp.where(lane == LANES - 1, last, 0.0)

    def traces(e):
        h, l = high.at[e % 2], low.at[e % 2]
        body = slice(N, (S + 1) * N)
        t = mm(pick_t[...], h[body, :]) + mm(pick_t[...], l[body, :])
        return to_row(jnp.sum(t * where_x[...], axis=1, keepdims=True))

    def fold(v):
        v = jnp.sum(v, axis=0, keepdims=True)
        return functools.reduce(lambda a, b: a + b, [v[:, i : i + LANES] for i in range(0, X, LANES)])

    def products(pairs):
        res = []
        for a, b in pairs:
            acc = None
            for s in range(S):
                t = a[own(s), :] * b[own(s), :]
                acc = t if acc is None else acc + t
            res.append(fold(acc))
        return res

    d = to_column(disp0[...])
    for sub in range(SUBITERS):
        er, ew = 2 * sub, 2 * sub + 1
        r, w, u = fields.at[er], fields.at[ew], fields.at[2 * SUBITERS]
        dh, dl = split(d * where_x[...])
        push = jnp.concatenate([dh, dl], axis=0)
        for s in range(S):
            r[own(s), :] = base[s * N : (s + 1) * N, :] + mm(pick[s * N : (s + 1) * N, :], push)
        if sub == 0:
            pl.semaphore_wait(barrier, nxs + nsp - 2)
        copies = start_halo(er)
        apply(er, w, copies)
        copies = start_halo(ew)
        rt, wt = traces(er), traces(ew)
        rr, rw, ww = products([(r, r), (r, w), (w, w)])
        apply(ew, u, copies)
        ru, wu, uu = products([(r, u), (w, u), (u, u)])
        mine = jnp.concatenate([rt, wt, rr, rw, ru, ww, wu, uu], axis=0)
        part[sub] = mine
        copies = []
        for o in range(1, nxs):
            c = pltpu.make_async_remote_copy(
                src_ref=part.at[sub], dst_ref=part_in.at[sub, xs],
                send_sem=xs_send.at[sub, o], recv_sem=xs_recv.at[sub, o],
                device_id={"xs": lax.rem(xs + o, nxs)}, device_id_type=MESH)
            c.start()
            copies.append(c)
            sent.append(c)
        part_in[sub, xs] = mine
        for c in copies:
            c.wait_recv()
        acc = part_in[sub, 0]
        for i in range(1, nxs):
            acc = acc + part_in[sub, i]
        total[sub] = acc
        copies = []
        for o in range(1, nsp):
            c = pltpu.make_async_remote_copy(
                src_ref=total.at[sub], dst_ref=total_in.at[sub, sp],
                send_sem=sp_send.at[sub, o], recv_sem=sp_recv.at[sub, o],
                device_id={"span": lax.rem(sp + o, nsp)}, device_id_type=MESH)
            c.start()
            copies.append(c)
            sent.append(c)
        total_in[sub, sp] = acc
        y = []
        for j in range(2):
            a = jnp.zeros((comp.shape[0], K), f32)
            for i in range(nxs):
                a = a + comp[:, i * K : (i + 1) * K] * part_in[sub, i, j : j + 1, :]
            y.append(jnp.sum(a, axis=1, keepdims=True))
        for c in copies:
            c.wait_recv()
        acc = total_in[sub, 0]
        for i in range(1, nsp):
            acc = acc + total_in[sub, i]
        g = jnp.sum(acc, axis=1, keepdims=True)
        rr, rw, ru, ww, wu, uu = [g[i : i + 1, :] for i in range(2, 8)]
        c0 = SHIFT
        g11 = ww + 2.0 * c0 * rw + c0 * c0 * rr
        g12 = wu + c0 * (ww + ru) + c0 * c0 * rw
        g22 = uu + 2.0 * c0 * wu + c0 * c0 * ww
        b1 = rw + c0 * rr
        b2 = ru + c0 * rw
        det = g11 * g22 - g12 * g12
        ca = (b1 * g22 - b2 * g12) / det
        cb = (b2 * g11 - b1 * g12) / det
        d = 0.5 * (ca * y[0] + cb * y[1]) + 0.5 * d
    for s in range(S):
        out[s * N : (s + 1) * N, :] = ca * r[own(s), :] + cb * w[own(s), :]
    dout[...] = to_row(d)
    for c in sent:
        c.wait_send()


def body(nsp, nxs, source, coefficient, volume, slo, sup, clo, cup, interface, compliance, start):
    N, S, X = source.shape
    K = interface.shape[2]
    M = compliance.shape[1]
    E = 2 * SUBITERS
    vm = pl.BlockSpec(memory_space=pltpu.VMEM)
    tall = (S + 2) * N
    dma = pltpu.SemaphoreType.DMA
    out, disp = pl.pallas_call(
        functools.partial(window, (nsp, nxs, N, S, X, K)),
        out_shape=(jax.ShapeDtypeStruct((S * N, X), f32), jax.ShapeDtypeStruct((1, K), f32)),
        in_specs=[vm] * 10,
        out_specs=(vm, vm),
        scratch_shapes=[
            pltpu.VMEM((6 * N, 3 * N), bf16),
            pltpu.VMEM((2, 2, N, N), bf16),
            pltpu.VMEM((S * N, X), f32),
            pltpu.VMEM((S * N, X), f32),
            pltpu.VMEM((E + 1, tall, X), f32),
            pltpu.VMEM((2, tall, X), bf16),
            pltpu.VMEM((2, tall, X), bf16),
            pltpu.VMEM((S * N, 2 * K), bf16),
            pltpu.VMEM((K, S * N), bf16),
            pltpu.VMEM((K, X), f32),
            pltpu.VMEM((E, 2, N, LANES), f32),
            pltpu.VMEM((E, 2, N, LANES), f32),
            pltpu.VMEM((SUBITERS, 8, LANES), f32),
            pltpu.VMEM((SUBITERS, nxs, 8, LANES), f32),
            pltpu.VMEM((SUBITERS, 8, LANES), f32),
            pltpu.VMEM((SUBITERS, nsp, 8, LANES), f32),
            dma((E, 4)), dma((E, 4)),
            dma((SUBITERS, nxs)), dma((SUBITERS, nxs)),
            dma((SUBITERS, nsp)), dma((SUBITERS, nsp)),
        ],
        compiler_params=pltpu.CompilerParams(
            collective_id=0, has_side_effects=True, vmem_limit_bytes=40 * 1024 * 1024),
        cost_estimate=pl.CostEstimate(flops=2 ** 30, bytes_accessed=2 ** 21, transcendentals=0),
        name="coupling_window",
    )(source, coefficient, volume, slo, sup, clo, cup,
      interface.reshape(1, K), compliance.reshape(M, compliance.shape[2]), start.reshape(1, K))
    return out.reshape(S, N, X).transpose(1, 0, 2), disp.reshape(1, 1, K)


def solution(mesh):
    field, shell = P(None, "span", "xs"), P("span", "xs", None)
    return jax.shard_map(
        functools.partial(body, mesh.shape["span"], mesh.shape["xs"]),
        mesh=mesh,
        in_specs=(field, field, P(), P(), P(), P(), P(), shell, shell, shell),
        out_specs=(field, shell),
        check_vma=False,
    )
```

```python
import functools

import jax
import jax.numpy as jnp
from jax import lax
from jax.experimental import pallas as pl
from jax.experimental.pallas import tpu as pltpu
from jax.sharding import PartitionSpec as P

SUBITERS = 2
SHIFT = 3.75
LANES = 128
MESH = pl.DeviceIdType.MESH
f32, bf16 = jnp.float32, jnp.bfloat16


def split(value):
    high = value.astype(bf16)
    return high, (value - high.astype(f32)).astype(bf16)


def mm(a, b):
    return jnp.dot(a, b, preferred_element_type=f32)


def iota(shape, dim):
    return lax.broadcasted_iota(jnp.int32, shape, dim)


def to_column(row):
    k = row.shape[1]
    wide = jnp.broadcast_to(row, (k, k))
    keep = iota((k, k), 0) == iota((k, k), 1)
    return jnp.sum(jnp.where(keep, wide, jnp.zeros_like(wide)), axis=1, keepdims=True)


def to_row(column):
    k = column.shape[0]
    wide = jnp.broadcast_to(column, (k, k))
    keep = iota((k, k), 0) == iota((k, k), 1)
    return jnp.sum(jnp.where(keep, wide, jnp.zeros_like(wide)), axis=0, keepdims=True)


def window(dims, *refs):
    given, refs = refs[:10], refs[10:]
    out, dout, refs = refs[0], refs[1], refs[2:]
    held, refs = refs[:10], refs[10:]
    run_window(dims, given, held, out, dout, *refs)


def run_window(dims, given, held, out, dout, big, side, cs, base, fields, high, low, pick, pick_t, where_x,
           col_out, col_in, part, part_in, total, total_in,
           halo_send, halo_recv, xs_send, xs_recv, sp_send, sp_recv,
           note_out, note_in, in_sem, out_sem):
    src, coef, vol, slo, sup, clo, cup, face, comp, disp0 = held
    fetch = [pltpu.make_async_copy(a, b, in_sem.at[i]) for i, (a, b) in enumerate(zip(given, held))]
    for i in (0, 7, 9, 2, 3, 4, 5, 6, 1, 8):
        fetch[i].start()
    nsp, nxs, N, S, X, K = dims
    sp, xs = lax.axis_index("span"), lax.axis_index("xs")
    barrier = pltpu.get_barrier_semaphore()
    for o in range(1, nxs):
        pl.semaphore_signal(barrier, inc=1, device_id={"xs": lax.rem(xs + o, nxs)}, device_id_type=MESH)
    for o in range(1, nsp):
        pl.semaphore_signal(barrier, inc=1, device_id={"span": lax.rem(sp + o, nsp)}, device_id_type=MESH)

    for i in (2, 3, 4, 5, 6, 7, 9):
        fetch[i].wait()

    zero = jnp.zeros((N, N), f32)
    rows = jnp.concatenate([
        jnp.concatenate([-slo[...], vol[...], -sup[...]], axis=1),
        jnp.concatenate([zero, clo[...], zero], axis=1),
        jnp.concatenate([zero, cup[...], zero], axis=1),
    ], axis=0)
    bh, bl = split(rows)
    big[: 3 * N, :] = bh
    big[3 * N :, :] = bl
    for i, m in enumerate((clo, cup)):
        mh, ml = split(m[...])
        side[i, 0] = mh
        side[i, 1] = ml

    index_row = face[...]
    index_col = to_column(index_row.astype(f32)).astype(jnp.int32)

    shift_x, shift_s = X.bit_length() - 1, S.bit_length() - 1

    def row_of(index):
        s = (index >> shift_x) & (S - 1)
        return s * N + (index >> (shift_x + shift_s))

    hot = (iota((S * N, K), 0) == row_of(index_row)).astype(f32).astype(bf16)
    pick[:, :K] = hot
    pick[:, K:] = hot
    pick_t[...] = (iota((K, S * N), 1) == row_of(index_col)).astype(f32).astype(bf16)
    where_x[...] = (iota((K, X), 1) == (index_col & (X - 1))).astype(f32)

    fetch[0].wait()
    fetch[1].wait()
    for s in range(S):
        base[s * N : (s + 1) * N, :] = src[:, s, :]
        cs[s * N : (s + 1) * N, :] = coef[:, s, :] - SHIFT

    lane = iota((N, LANES), 1)
    wide = iota((N, X), 1)
    sent = []

    def own(s):
        return slice((s + 1) * N, (s + 2) * N)

    def own_ds(s):
        return pl.ds((s + 1) * N, N)

    up, down = lax.rem(sp + 1, nsp), lax.rem(sp + nsp - 1, nsp)
    right, left = lax.rem(xs + 1, nxs), lax.rem(xs + nxs - 1, nxs)
    towards = (("span", up), ("span", down), ("xs", right), ("xs", left))
    order = [0, S - 1] + list(range(1, S - 1))

    def send(e, i, from_ref, to_ref):
        axis, target = towards[i]
        c = pltpu.make_async_remote_copy(
            src_ref=from_ref, dst_ref=to_ref, send_sem=halo_send.at[e, i], recv_sem=halo_recv.at[e, i],
            device_id={axis: target}, device_id_type=MESH)
        c.start()
        sent.append(c)
        return c

    def split_own(e, s):
        high[e % 2, own(s), :], low[e % 2, own(s), :] = split(fields[e, own(s), :])

    def split_halo(e):
        for row in (slice(0, N), slice((S + 1) * N, (S + 2) * N)):
            high[e % 2, row, :], low[e % 2, row, :] = split(fields[e, row, :])

    def start_halo(e, fill):
        f = fields.at[e]
        fill(0)
        fill(S - 1)
        if e == 0:
            pl.semaphore_wait(barrier, nxs + nsp - 2)
        copies = [
            send(e, 0, f.at[pl.ds(S * N, N)], f.at[pl.ds(0, N)]),
            send(e, 1, f.at[pl.ds(N, N)], f.at[pl.ds((S + 1) * N, N)]),
        ]
        first = jnp.zeros((N, LANES), f32)
        last = jnp.zeros((N, LANES), f32)
        for s in order:
            if 0 < s < S - 1:
                fill(s)
            a = f[own(s), :LANES]
            b = f[own(s), X - LANES :]
            first = jnp.where(lane == s, pltpu.roll(a, s, 1) if s else a, first)
            last = jnp.where(lane == s, pltpu.roll(b, s + 1, 1), last)
        col_out[e, 0] = first
        col_out[e, 1] = last
        copies.append(send(e, 2, col_out.at[e, 1], col_in.at[e, 0]))
        copies.append(send(e, 3, col_out.at[e, 0], col_in.at[e, 1]))
        for s in range(S):
            split_own(e, s)

        def finish():
            for c in copies:
                c.wait_recv()
            split_halo(e)

        return finish

    def start_change(e, change, fill):
        note_out[e // 2] = jnp.concatenate(
            [index_row.astype(f32), to_row(change), jnp.zeros((6, K), f32)], axis=0)
        copies = [send(e, i, note_out.at[e // 2], note_in.at[e // 2, i]) for i in range(4)]
        for s in range(S):
            fill(s)
            split_own(e, s)

        def finish():
            for c in copies:
                c.wait_recv()
            for i in range(4):
                there = note_in[e // 2, i]
                at_row = there[0:1].astype(jnp.int32)
                at = to_column(there[0:1]).astype(jnp.int32)
                by = to_column(there[1:2])
                if i < 2:
                    s, halo = ((S - 1, 0), (0, S + 1))[i]
                    hot = (iota((N, K), 0) + s * N == row_of(at_row)).astype(f32).astype(bf16)
                    vh, vl = split(jnp.where(iota((K, X), 1) == (at & (X - 1)), by, 0.0))
                    halo = slice(halo * N, (halo + 1) * N)
                    fields[e, halo, :] = fields[e - 2, halo, :] + (mm(hot, vh) + mm(hot, vl))
                else:
                    edge = (X - 1, 0)[i - 2]
                    node = at_row >> (shift_x + shift_s)
                    hot = (iota((N, K), 0) == node).astype(f32).astype(bf16)
                    by = jnp.where((at & (X - 1)) == edge, by, 0.0)
                    s_of = (at >> shift_x) & (S - 1)
                    vh, vl = split(jnp.where(iota((K, LANES), 1) == s_of, by, 0.0))
                    col_in[e, i - 2] = col_in[e - 2, i - 2] + (mm(hot, vh) + mm(hot, vl))
            split_halo(e)

        return finish

    def apply(e, target, finish):
        f, h, l = fields.at[e], high.at[e % 2], low.at[e % 2]

        def element_row(s):
            near = slice(s * N, (s + 3) * N)
            xh, xl = h[near, :], l[near, :]
            p = mm(big[...], xh)
            r = p[: 3 * N] + p[3 * N :] + mm(big[: 3 * N, :], xl)
            res = cs[s * N : (s + 1) * N, :] * f[own(s), :] + r[:N]
            res = res - jnp.where(wide == 0, 0.0, pltpu.roll(r[N : 2 * N], 1, 1))
            res = res - jnp.where(wide == X - 1, 0.0, pltpu.roll(r[2 * N :], X - 1, 1))
            target[own(s), :] = res

        for s in range(1, S - 1):
            element_row(s)
        finish()
        element_row(0)
        element_row(S - 1)
        edges = []
        for i, there in enumerate((xs > 0, xs < nxs - 1)):
            got = jnp.where(there, col_in[e, i], 0.0)
            gh, gl = split(got)
            edges.append(mm(side[i, 0], gh) + mm(side[i, 1], gh) + mm(side[i, 0], gl))

        def fill(s):
            first = pltpu.roll(edges[0], LANES - s, 1) if s else edges[0]
            target[own(s), :LANES] = target[own(s), :LANES] - jnp.where(lane == 0, first, 0.0)
            last = pltpu.roll(edges[1], LANES - 1 - s, 1)
            target[own(s), X - LANES :] = target[own(s), X - LANES :] - jnp.where(lane == LANES - 1, last, 0.0)

        return fill

    def traces(e):
        h, l = high.at[e % 2], low.at[e % 2]
        body = slice(N, (S + 1) * N)
        t = mm(pick_t[...], h[body, :]) + mm(pick_t[...], l[body, :])
        return to_row(jnp.sum(t * where_x[...], axis=1, keepdims=True))

    def fold(v):
        v = jnp.sum(v, axis=0, keepdims=True)
        return functools.reduce(lambda a, b: a + b, [v[:, i : i + LANES] for i in range(0, X, LANES)])

    def products(pairs):
        res = []
        for a, b in pairs:
            acc = None
            for s in range(S):
                t = a[own(s), :] * b[own(s), :]
                acc = t if acc is None else acc + t
            res.append(fold(acc))
        return res

    d = to_column(disp0[...])
    for sub in range(SUBITERS):
        er, ew = 2 * sub, 2 * sub + 1
        r, w, u = fields.at[er], fields.at[ew], fields.at[2 * SUBITERS]
        dh, dl = split(d * where_x[...])
        push = jnp.concatenate([dh, dl], axis=0)

        def fill_rhs(s):
            r[own(s), :] = base[s * N : (s + 1) * N, :] + mm(pick[s * N : (s + 1) * N, :], push)

        finish = start_change(er, change, fill_rhs) if sub else start_halo(er, fill_rhs)
        finish = start_halo(ew, apply(er, w, finish))
        rt, wt = traces(er), traces(ew)
        rr, rw, ww = products([(r, r), (r, w), (w, w)])
        fill = apply(ew, u, finish)
        for s in range(S):
            fill(s)
        ru, wu, uu = products([(r, u), (w, u), (u, u)])
        mine = jnp.concatenate([rt, wt, rr, rw, ru, ww, wu, uu], axis=0)
        part[sub] = mine
        copies = []
        for o in range(1, nxs):
            c = pltpu.make_async_remote_copy(
                src_ref=part.at[sub], dst_ref=part_in.at[sub, xs],
                send_sem=xs_send.at[sub, o], recv_sem=xs_recv.at[sub, o],
                device_id={"xs": lax.rem(xs + o, nxs)}, device_id_type=MESH)
            c.start()
            copies.append(c)
            sent.append(c)
        part_in[sub, xs] = mine
        for c in copies:
            c.wait_recv()
        acc = part_in[sub, 0]
        for i in range(1, nxs):
            acc = acc + part_in[sub, i]
        total[sub] = acc
        copies = []
        for o in range(1, nsp):
            c = pltpu.make_async_remote_copy(
                src_ref=total.at[sub], dst_ref=total_in.at[sub, sp],
                send_sem=sp_send.at[sub, o], recv_sem=sp_recv.at[sub, o],
                device_id={"span": lax.rem(sp + o, nsp)}, device_id_type=MESH)
            c.start()
            copies.append(c)
            sent.append(c)
        total_in[sub, sp] = acc
        if sub == 0:
            fetch[8].wait()
        y = []
        for j in range(2):
            a = jnp.zeros((comp.shape[0], K), f32)
            for i in range(nxs):
                a = a + comp[:, i * K : (i + 1) * K] * part_in[sub, i, j : j + 1, :]
            y.append(jnp.sum(a, axis=1, keepdims=True))
        for c in copies:
            c.wait_recv()
        acc = total_in[sub, 0]
        for i in range(1, nsp):
            acc = acc + total_in[sub, i]
        g = jnp.sum(acc, axis=1, keepdims=True)
        rr, rw, ru, ww, wu, uu = [g[i : i + 1, :] for i in range(2, 8)]
        c0 = SHIFT
        g11 = ww + 2.0 * c0 * rw + c0 * c0 * rr
        g12 = wu + c0 * (ww + ru) + c0 * c0 * rw
        g22 = uu + 2.0 * c0 * wu + c0 * c0 * ww
        b1 = rw + c0 * rr
        b2 = ru + c0 * rw
        det = g11 * g22 - g12 * g12
        ca = (b1 * g22 - b2 * g12) / det
        cb = (b2 * g11 - b1 * g12) / det
        change = 0.5 * (ca * y[0] + cb * y[1]) - 0.5 * d
        d = 0.5 * (ca * y[0] + cb * y[1]) + 0.5 * d
    leaving = []
    for s in range(S):
        u[own(s), :] = ca * r[own(s), :] + cb * w[own(s), :]
        c = pltpu.make_async_copy(u.at[own_ds(s)], out.at[pl.ds(s * N, N)], out_sem.at[s])
        c.start()
        leaving.append(c)
    dout[...] = to_row(d)
    for c in sent:
        c.wait_send()
    for c in leaving:
        c.wait()


def body(nsp, nxs, source, coefficient, volume, slo, sup, clo, cup, interface, compliance, start):
    N, S, X = source.shape
    K = interface.shape[2]
    M = compliance.shape[1]
    E = 2 * SUBITERS
    vm = pl.BlockSpec(memory_space=pltpu.VMEM)
    hbm = pl.BlockSpec(memory_space=pltpu.HBM)
    tall = (S + 2) * N
    dma = pltpu.SemaphoreType.DMA
    args = (source, coefficient, volume, slo, sup, clo, cup,
            interface.reshape(1, K), compliance.reshape(M, compliance.shape[2]), start.reshape(1, K))
    out, disp = pl.pallas_call(
        functools.partial(window, (nsp, nxs, N, S, X, K)),
        out_shape=(jax.ShapeDtypeStruct((S * N, X), f32), jax.ShapeDtypeStruct((1, K), f32)),
        in_specs=[hbm] * 10,
        out_specs=(hbm, vm),
        scratch_shapes=[pltpu.VMEM(a.shape, a.dtype) for a in args] + [
            pltpu.VMEM((6 * N, 3 * N), bf16),
            pltpu.VMEM((2, 2, N, N), bf16),
            pltpu.VMEM((S * N, X), f32),
            pltpu.VMEM((S * N, X), f32),
            pltpu.VMEM((E + 1, tall, X), f32),
            pltpu.VMEM((2, tall, X), bf16),
            pltpu.VMEM((2, tall, X), bf16),
            pltpu.VMEM((S * N, 2 * K), bf16),
            pltpu.VMEM((K, S * N), bf16),
            pltpu.VMEM((K, X), f32),
            pltpu.VMEM((E, 2, N, LANES), f32),
            pltpu.VMEM((E, 2, N, LANES), f32),
            pltpu.VMEM((SUBITERS, 8, LANES), f32),
            pltpu.VMEM((SUBITERS, nxs, 8, LANES), f32),
            pltpu.VMEM((SUBITERS, 8, LANES), f32),
            pltpu.VMEM((SUBITERS, nsp, 8, LANES), f32),
            dma((E, 4)), dma((E, 4)),
            dma((SUBITERS, nxs)), dma((SUBITERS, nxs)),
            dma((SUBITERS, nsp)), dma((SUBITERS, nsp)),
            pltpu.VMEM((SUBITERS, 8, K), f32),
            pltpu.VMEM((SUBITERS, 4, 8, K), f32),
            dma((10,)), dma((S,)),
        ],
        compiler_params=pltpu.CompilerParams(
            collective_id=0, has_side_effects=True, vmem_limit_bytes=40 * 1024 * 1024),
        cost_estimate=pl.CostEstimate(flops=2 ** 30, bytes_accessed=2 ** 21, transcendentals=0),
        name="coupling_window",
    )(*args)
    return out.reshape(S, N, X).transpose(1, 0, 2), disp.reshape(1, 1, K)


def solution(mesh):
    field, shell = P(None, "span", "xs"), P("span", "xs", None)
    return jax.shard_map(
        functools.partial(body, mesh.shape["span"], mesh.shape["xs"]),
        mesh=mesh,
        in_specs=(field, field, P(), P(), P(), P(), P(), shell, shell, shell),
        out_specs=(field, shell),
        check_vma=False,
    )
```

```python
import functools

import jax
import jax.numpy as jnp
from jax import lax
from jax.experimental import pallas as pl
from jax.experimental.pallas import tpu as pltpu
from jax.sharding import PartitionSpec as P

SUBITERS = 2
SHIFT = 3.75
LANES = 128
MESH = pl.DeviceIdType.MESH
f32, bf16 = jnp.float32, jnp.bfloat16


def split(value):
    high = value.astype(bf16)
    return high, (value - high.astype(f32)).astype(bf16)


def mm(a, b):
    return jnp.dot(a, b, preferred_element_type=f32)


def iota(shape, dim):
    return lax.broadcasted_iota(jnp.int32, shape, dim)


def to_column(row):
    k = row.shape[1]
    wide = jnp.broadcast_to(row, (k, k))
    keep = iota((k, k), 0) == iota((k, k), 1)
    return jnp.sum(jnp.where(keep, wide, jnp.zeros_like(wide)), axis=1, keepdims=True)


def to_row(column):
    k = column.shape[0]
    wide = jnp.broadcast_to(column, (k, k))
    keep = iota((k, k), 0) == iota((k, k), 1)
    return jnp.sum(jnp.where(keep, wide, jnp.zeros_like(wide)), axis=0, keepdims=True)


def window(dims, *refs):
    given, refs = refs[:10], refs[10:]
    out, dout, refs = refs[0], refs[1], refs[2:]
    held, refs = refs[:10], refs[10:]
    run_window(dims, given, held, out, dout, *refs)


def run_window(dims, given, held, out, dout, big, side, cs, base, fields, high, low, pick, pick_t, where_x,
           col_out, col_in, part, part_in, total, total_in,
           halo_send, halo_recv, xs_send, xs_recv, sp_send, sp_recv,
           note_out, note_in, in_sem, out_sem):
    src, coef, vol, slo, sup, clo, cup, face, comp, disp0 = held
    fetch = [pltpu.make_async_copy(a, b, in_sem.at[i]) for i, (a, b) in enumerate(zip(given, held))]
    for i in (0, 7, 9, 2, 3, 4, 5, 6, 1, 8):
        fetch[i].start()
    nsp, nxs, N, S, X, K = dims
    sp, xs = lax.axis_index("span"), lax.axis_index("xs")
    barrier = pltpu.get_barrier_semaphore()
    for o in range(1, nxs):
        pl.semaphore_signal(barrier, inc=1, device_id={"xs": lax.rem(xs + o, nxs)}, device_id_type=MESH)
    for o in range(1, nsp):
        pl.semaphore_signal(barrier, inc=1, device_id={"span": lax.rem(sp + o, nsp)}, device_id_type=MESH)

    for i in (2, 3, 4, 5, 6, 7, 9):
        fetch[i].wait()

    zero = jnp.zeros((N, N), f32)
    rows = jnp.concatenate([
        jnp.concatenate([-slo[...], vol[...], -sup[...]], axis=1),
        jnp.concatenate([zero, clo[...], zero], axis=1),
        jnp.concatenate([zero, cup[...], zero], axis=1),
    ], axis=0)
    bh, bl = split(rows)
    big[: 3 * N, :] = bh
    big[3 * N :, :] = bl
    for i, m in enumerate((clo, cup)):
        mh, ml = split(m[...])
        side[i, 0] = mh
        side[i, 1] = ml

    index_row = face[...]
    index_col = to_column(index_row.astype(f32)).astype(jnp.int32)

    shift_x, shift_s = X.bit_length() - 1, S.bit_length() - 1

    def row_of(index):
        s = (index >> shift_x) & (S - 1)
        return s * N + (index >> (shift_x + shift_s))

    hot = (iota((S * N, K), 0) == row_of(index_row)).astype(f32).astype(bf16)
    pick[:, :K] = hot
    pick[:, K:] = hot
    pick_t[...] = (iota((K, S * N), 1) == row_of(index_col)).astype(f32).astype(bf16)
    where_x[...] = (iota((K, X), 1) == (index_col & (X - 1))).astype(f32)

    fetch[0].wait()
    fetch[1].wait()
    for s in range(S):
        base[s * N : (s + 1) * N, :] = src[:, s, :]
        cs[s * N : (s + 1) * N, :] = coef[:, s, :] - SHIFT

    lane = iota((N, LANES), 1)
    wide = iota((N, X), 1)
    sent = []

    def own(s):
        return slice((s + 1) * N, (s + 2) * N)

    def own_ds(s):
        return pl.ds((s + 1) * N, N)

    up, down = lax.rem(sp + 1, nsp), lax.rem(sp + nsp - 1, nsp)
    right, left = lax.rem(xs + 1, nxs), lax.rem(xs + nxs - 1, nxs)
    towards = (("span", up), ("span", down), ("xs", right), ("xs", left))
    order = [0, S - 1] + list(range(1, S - 1))

    def send(e, i, from_ref, to_ref):
        axis, target = towards[i]
        c = pltpu.make_async_remote_copy(
            src_ref=from_ref, dst_ref=to_ref, send_sem=halo_send.at[e, i], recv_sem=halo_recv.at[e, i],
            device_id={axis: target}, device_id_type=MESH)
        c.start()
        sent.append(c)
        return c

    def split_own(e, s):
        high[e % 2, own(s), :], low[e % 2, own(s), :] = split(fields[e, own(s), :])

    def split_halo(e):
        for row in (slice(0, N), slice((S + 1) * N, (S + 2) * N)):
            high[e % 2, row, :], low[e % 2, row, :] = split(fields[e, row, :])

    def start_halo(e, fill):
        f = fields.at[e]
        fill(0)
        fill(S - 1)
        if e == 0:
            pl.semaphore_wait(barrier, nxs + nsp - 2)
        copies = [
            send(e, 0, f.at[pl.ds(S * N, N)], f.at[pl.ds(0, N)]),
            send(e, 1, f.at[pl.ds(N, N)], f.at[pl.ds((S + 1) * N, N)]),
        ]
        first = jnp.zeros((N, LANES), f32)
        last = jnp.zeros((N, LANES), f32)
        for s in order:
            if 0 < s < S - 1:
                fill(s)
            a = f[own(s), :LANES]
            b = f[own(s), X - LANES :]
            first = jnp.where(lane == s, pltpu.roll(a, s, 1) if s else a, first)
            last = jnp.where(lane == s, pltpu.roll(b, s + 1, 1), last)
        col_out[e, 0] = first
        col_out[e, 1] = last
        copies.append(send(e, 2, col_out.at[e, 1], col_in.at[e, 0]))
        copies.append(send(e, 3, col_out.at[e, 0], col_in.at[e, 1]))
        for s in range(S):
            split_own(e, s)

        def finish():
            for c in copies:
                c.wait_recv()
            split_halo(e)

        return finish

    def start_change(e, change, fill):
        note_out[e // 2] = jnp.concatenate(
            [index_row.astype(f32), to_row(change), jnp.zeros((6, K), f32)], axis=0)
        copies = [send(e, i, note_out.at[e // 2], note_in.at[e // 2, i]) for i in range(4)]
        for s in range(S):
            fill(s)
            split_own(e, s)

        def finish():
            for c in copies:
                c.wait_recv()
            for i in range(4):
                there = note_in[e // 2, i]
                at_row = there[0:1].astype(jnp.int32)
                at = to_column(there[0:1]).astype(jnp.int32)
                by = to_column(there[1:2])
                if i < 2:
                    s, halo = ((S - 1, 0), (0, S + 1))[i]
                    hot = (iota((N, K), 0) + s * N == row_of(at_row)).astype(f32).astype(bf16)
                    vh, vl = split(jnp.where(iota((K, X), 1) == (at & (X - 1)), by, 0.0))
                    halo = slice(halo * N, (halo + 1) * N)
                    fields[e, halo, :] = fields[e - 2, halo, :] + (mm(hot, vh) + mm(hot, vl))
                else:
                    edge = (X - 1, 0)[i - 2]
                    node = at_row >> (shift_x + shift_s)
                    hot = (iota((N, K), 0) == node).astype(f32).astype(bf16)
                    by = jnp.where((at & (X - 1)) == edge, by, 0.0)
                    s_of = (at >> shift_x) & (S - 1)
                    vh, vl = split(jnp.where(iota((K, LANES), 1) == s_of, by, 0.0))
                    col_in[e, i - 2] = col_in[e - 2, i - 2] + (mm(hot, vh) + mm(hot, vl))
            split_halo(e)

        return finish

    def apply(e, target, finish):
        f, h, l = fields.at[e], high.at[e % 2], low.at[e % 2]

        def element_row(s):
            near = slice(s * N, (s + 3) * N)
            xh, xl = h[near, :], l[near, :]
            p = mm(big[...], xh)
            r = p[: 3 * N] + p[3 * N :] + mm(big[: 3 * N, :], xl)
            res = cs[s * N : (s + 1) * N, :] * f[own(s), :] + r[:N]
            res = res - jnp.where(wide == 0, 0.0, pltpu.roll(r[N : 2 * N], 1, 1))
            res = res - jnp.where(wide == X - 1, 0.0, pltpu.roll(r[2 * N :], X - 1, 1))
            target[own(s), :] = res

        for s in range(1, S - 1):
            element_row(s)
        finish()
        element_row(0)
        element_row(S - 1)
        edges = []
        for i, there in enumerate((xs > 0, xs < nxs - 1)):
            got = jnp.where(there, col_in[e, i], 0.0)
            gh, gl = split(got)
            edges.append(mm(side[i, 0], gh) + mm(side[i, 1], gh) + mm(side[i, 0], gl))

        def fill(s):
            first = pltpu.roll(edges[0], LANES - s, 1) if s else edges[0]
            target[own(s), :LANES] = target[own(s), :LANES] - jnp.where(lane == 0, first, 0.0)
            last = pltpu.roll(edges[1], LANES - 1 - s, 1)
            target[own(s), X - LANES :] = target[own(s), X - LANES :] - jnp.where(lane == LANES - 1, last, 0.0)

        return fill

    def traces(e):
        h, l = high.at[e % 2], low.at[e % 2]
        body = slice(N, (S + 1) * N)
        t = mm(pick_t[...], h[body, :]) + mm(pick_t[...], l[body, :])
        return to_row(jnp.sum(t * where_x[...], axis=1, keepdims=True))

    def fold(v):
        v = jnp.sum(v, axis=0, keepdims=True)
        return functools.reduce(lambda a, b: a + b, [v[:, i : i + LANES] for i in range(0, X, LANES)])

    def products(pairs):
        res = []
        for a, b in pairs:
            acc = None
            for s in range(S):
                t = a[own(s), :] * b[own(s), :]
                acc = t if acc is None else acc + t
            res.append(fold(acc))
        return res

    d = to_column(disp0[...])
    for sub in range(SUBITERS):
        er, ew = 2 * sub, 2 * sub + 1
        r, w, u = fields.at[er], fields.at[ew], fields.at[2 * SUBITERS]
        dh, dl = split(d * where_x[...])
        push = jnp.concatenate([dh, dl], axis=0)

        def fill_rhs(s):
            r[own(s), :] = base[s * N : (s + 1) * N, :] + mm(pick[s * N : (s + 1) * N, :], push)

        finish = start_change(er, change, fill_rhs) if sub else start_halo(er, fill_rhs)
        finish = start_halo(ew, apply(er, w, finish))
        rt, wt = traces(er), traces(ew)
        rr, rw, ww = products([(r, r), (r, w), (w, w)])
        fill = apply(ew, u, finish)
        for s in range(S):
            fill(s)
        ru, wu, uu = products([(r, u), (w, u), (u, u)])
        mine = jnp.concatenate([rt, wt, rr, rw, ru, ww, wu, uu], axis=0)
        part[sub] = mine
        copies = []
        for o in range(1, nxs):
            c = pltpu.make_async_remote_copy(
                src_ref=part.at[sub], dst_ref=part_in.at[sub, xs],
                send_sem=xs_send.at[sub, o], recv_sem=xs_recv.at[sub, o],
                device_id={"xs": lax.rem(xs + o, nxs)}, device_id_type=MESH)
            c.start()
            copies.append(c)
            sent.append(c)
        part_in[sub, xs] = mine
        for c in copies:
            c.wait_recv()
        acc = part_in[sub, 0]
        for i in range(1, nxs):
            acc = acc + part_in[sub, i]
        total[sub] = acc
        copies = []
        for o in range(1, nsp):
            c = pltpu.make_async_remote_copy(
                src_ref=total.at[sub], dst_ref=total_in.at[sub, sp],
                send_sem=sp_send.at[sub, o], recv_sem=sp_recv.at[sub, o],
                device_id={"span": lax.rem(sp + o, nsp)}, device_id_type=MESH)
            c.start()
            copies.append(c)
            sent.append(c)
        total_in[sub, sp] = acc
        if sub == 0:
            fetch[8].wait()
        y = []
        for j in range(2):
            a = jnp.zeros((comp.shape[0], K), f32)
            for i in range(nxs):
                a = a + comp[:, i * K : (i + 1) * K] * part_in[sub, i, j : j + 1, :]
            y.append(jnp.sum(a, axis=1, keepdims=True))
        for c in copies:
            c.wait_recv()
        acc = total_in[sub, 0]
        for i in range(1, nsp):
            acc = acc + total_in[sub, i]
        g = jnp.sum(acc, axis=1, keepdims=True)
        rr, rw, ru, ww, wu, uu = [g[i : i + 1, :] for i in range(2, 8)]
        c0 = SHIFT
        g11 = ww + 2.0 * c0 * rw + c0 * c0 * rr
        g12 = wu + c0 * (ww + ru) + c0 * c0 * rw
        g22 = uu + 2.0 * c0 * wu + c0 * c0 * ww
        b1 = rw + c0 * rr
        b2 = ru + c0 * rw
        det = g11 * g22 - g12 * g12
        ca = (b1 * g22 - b2 * g12) / det
        cb = (b2 * g11 - b1 * g12) / det
        change = 0.5 * (ca * y[0] + cb * y[1]) - 0.5 * d
        d = 0.5 * (ca * y[0] + cb * y[1]) + 0.5 * d
    leaving = []
    for s in range(S):
        u[own(s), :] = ca * r[own(s), :] + cb * w[own(s), :]
        c = pltpu.make_async_copy(u.at[own_ds(s)], out.at[pl.ds(s * N, N)], out_sem.at[s])
        c.start()
        leaving.append(c)
    dout[...] = to_row(d)
    for c in sent:
        c.wait_send()
    for c in leaving:
        c.wait()


def body(nsp, nxs, source, coefficient, volume, slo, sup, clo, cup, interface, compliance, start):
    N, S, X = source.shape
    K = interface.shape[2]
    M = compliance.shape[1]
    E = 2 * SUBITERS
    vm = pl.BlockSpec(memory_space=pltpu.VMEM)
    hbm = pl.BlockSpec(memory_space=pltpu.HBM)
    tall = (S + 2) * N
    dma = pltpu.SemaphoreType.DMA
    args = (source, coefficient, volume, slo, sup, clo, cup,
            interface.reshape(1, K), compliance.reshape(M, compliance.shape[2]), start.reshape(1, K))
    out, disp = pl.pallas_call(
        functools.partial(window, (nsp, nxs, N, S, X, K)),
        out_shape=(jax.ShapeDtypeStruct((S * N, X), f32), jax.ShapeDtypeStruct((1, K), f32)),
        in_specs=[hbm] * 10,
        out_specs=(hbm, vm),
        scratch_shapes=[pltpu.VMEM(a.shape, a.dtype) for a in args] + [
            pltpu.VMEM((6 * N, 3 * N), bf16),
            pltpu.VMEM((2, 2, N, N), bf16),
            pltpu.VMEM((S * N, X), f32),
            pltpu.VMEM((S * N, X), f32),
            pltpu.VMEM((E + 1, tall, X), f32),
            pltpu.VMEM((2, tall, X), bf16),
            pltpu.VMEM((2, tall, X), bf16),
            pltpu.VMEM((S * N, 2 * K), bf16),
            pltpu.VMEM((K, S * N), bf16),
            pltpu.VMEM((K, X), f32),
            pltpu.VMEM((E, 2, N, LANES), f32),
            pltpu.VMEM((E, 2, N, LANES), f32),
            pltpu.VMEM((SUBITERS, 8, LANES), f32),
            pltpu.VMEM((SUBITERS, nxs, 8, LANES), f32),
            pltpu.VMEM((SUBITERS, 8, LANES), f32),
            pltpu.VMEM((SUBITERS, nsp, 8, LANES), f32),
            dma((E, 4)), dma((E, 4)),
            dma((SUBITERS, nxs)), dma((SUBITERS, nxs)),
            dma((SUBITERS, nsp)), dma((SUBITERS, nsp)),
            pltpu.VMEM((SUBITERS, 8, K), f32),
            pltpu.VMEM((SUBITERS, 4, 8, K), f32),
            dma((10,)), dma((S,)),
        ],
        compiler_params=pltpu.CompilerParams(
            collective_id=0, has_side_effects=True, vmem_limit_bytes=64 * 1024 * 1024),
        cost_estimate=pl.CostEstimate(flops=2 ** 30, bytes_accessed=2 ** 21, transcendentals=0),
        name="coupling_window",
    )(*args)
    return out.reshape(S, N, X).transpose(1, 0, 2), disp.reshape(1, 1, K)


def solution(mesh):
    field, shell = P(None, "span", "xs"), P("span", "xs", None)
    return jax.shard_map(
        functools.partial(body, mesh.shape["span"], mesh.shape["xs"]),
        mesh=mesh,
        in_specs=(field, field, P(), P(), P(), P(), P(), shell, shell, shell),
        out_specs=(field, shell),
        check_vma=False,
    )
```

```python
import functools

import jax
import jax.numpy as jnp
from jax import lax
from jax.experimental import pallas as pl
from jax.experimental.pallas import tpu as pltpu
from jax.sharding import PartitionSpec as P

SUBITERS = 2
SHIFT = 3.75
LANES = 128
MESH = pl.DeviceIdType.MESH
f32, bf16 = jnp.float32, jnp.bfloat16


def split(value):
    high = value.astype(bf16)
    return high, (value - high.astype(f32)).astype(bf16)


def mm(a, b):
    return jnp.dot(a, b, preferred_element_type=f32)


def iota(shape, dim):
    return lax.broadcasted_iota(jnp.int32, shape, dim)


def to_column(row):
    k = row.shape[1]
    wide = jnp.broadcast_to(row, (k, k))
    keep = iota((k, k), 0) == iota((k, k), 1)
    return jnp.sum(jnp.where(keep, wide, jnp.zeros_like(wide)), axis=1, keepdims=True)


def to_row(column):
    k = column.shape[0]
    wide = jnp.broadcast_to(column, (k, k))
    keep = iota((k, k), 0) == iota((k, k), 1)
    return jnp.sum(jnp.where(keep, wide, jnp.zeros_like(wide)), axis=0, keepdims=True)


def window(dims, *refs):
    given, refs = refs[:10], refs[10:]
    out, dout, refs = refs[0], refs[1], refs[2:]
    held, refs = refs[:10], refs[10:]
    run_window(dims, given, held, out, dout, *refs)


def run_window(dims, given, held, out, dout, big, side, cs, base, fields, high, low, pick, pick_t, where_x,
           col_out, col_in, part, part_in, total, total_in,
           halo_send, halo_recv, xs_send, xs_recv, sp_send, sp_recv,
           note_out, note_in, in_sem, out_sem):
    src, coef, vol, slo, sup, clo, cup, face, comp, disp0 = held
    fetch = [pltpu.make_async_copy(a, b, in_sem.at[i]) for i, (a, b) in enumerate(zip(given, held))]
    for i in (0, 7, 9, 2, 3, 4, 5, 6, 1, 8):
        fetch[i].start()
    nsp, nxs, N, S, X, K = dims
    sp, xs = lax.axis_index("span"), lax.axis_index("xs")
    barrier = pltpu.get_barrier_semaphore()
    for o in range(1, nxs):
        pl.semaphore_signal(barrier, inc=1, device_id={"xs": lax.rem(xs + o, nxs)}, device_id_type=MESH)
    for o in range(1, nsp):
        pl.semaphore_signal(barrier, inc=1, device_id={"span": lax.rem(sp + o, nsp)}, device_id_type=MESH)

    fetch[7].wait()
    fetch[9].wait()

    index_row = face[...]
    index_col = to_column(index_row.astype(f32)).astype(jnp.int32)

    shift_x, shift_s = X.bit_length() - 1, S.bit_length() - 1

    def row_of(index):
        s = (index >> shift_x) & (S - 1)
        return s * N + (index >> (shift_x + shift_s))

    place = row_of(index_row)
    where_x[...] = (iota((K, X), 1) == (index_col & (X - 1))).astype(f32)

    def prepare():
        for i in range(2, 7):
            fetch[i].wait()
        zero = jnp.zeros((N, N), f32)
        rows = jnp.concatenate([
            jnp.concatenate([-slo[...], vol[...], -sup[...]], axis=1),
            jnp.concatenate([zero, clo[...], zero], axis=1),
            jnp.concatenate([zero, cup[...], zero], axis=1),
        ], axis=0)
        bh, bl = split(rows)
        big[: 3 * N, :] = bh
        big[3 * N :, :] = bl
        for i, m in enumerate((clo, cup)):
            mh, ml = split(m[...])
            side[i, 0] = mh
            side[i, 1] = ml
        pick_t[...] = (iota((K, S * N), 1) == row_of(index_col)).astype(f32).astype(bf16)
        fetch[1].wait()
        for s in range(S):
            cs[s * N : (s + 1) * N, :] = coef[:, s, :] - SHIFT

    lane = iota((N, LANES), 1)
    wide = iota((N, X), 1)
    sent = []

    def own(s):
        return slice((s + 1) * N, (s + 2) * N)

    up, down = lax.rem(sp + 1, nsp), lax.rem(sp + nsp - 1, nsp)
    right, left = lax.rem(xs + 1, nxs), lax.rem(xs + nxs - 1, nxs)
    towards = (("span", up), ("span", down), ("xs", right), ("xs", left))
    order = [0, S - 1] + list(range(1, S - 1))

    def send(e, i, from_ref, to_ref):
        axis, target = towards[i]
        c = pltpu.make_async_remote_copy(
            src_ref=from_ref, dst_ref=to_ref, send_sem=halo_send.at[e, i], recv_sem=halo_recv.at[e, i],
            device_id={axis: target}, device_id_type=MESH)
        c.start()
        sent.append(c)
        return c

    def split_own(e, s):
        high[e % 2, own(s), :], low[e % 2, own(s), :] = split(fields[e, own(s), :])

    def split_halo(e):
        for row in (slice(0, N), slice((S + 1) * N, (S + 2) * N)):
            high[e % 2, row, :], low[e % 2, row, :] = split(fields[e, row, :])

    def start_halo(e, fill):
        f = fields.at[e]
        fill(0)
        fill(S - 1)
        if e == 0:
            pl.semaphore_wait(barrier, nxs + nsp - 2)
        copies = [
            send(e, 0, f.at[pl.ds(S * N, N)], f.at[pl.ds(0, N)]),
            send(e, 1, f.at[pl.ds(N, N)], f.at[pl.ds((S + 1) * N, N)]),
        ]
        first = jnp.zeros((N, LANES), f32)
        last = jnp.zeros((N, LANES), f32)
        for s in order:
            if 0 < s < S - 1:
                fill(s)
            a = f[own(s), :LANES]
            b = f[own(s), X - LANES :]
            first = jnp.where(lane == s, pltpu.roll(a, s, 1) if s else a, first)
            last = jnp.where(lane == s, pltpu.roll(b, s + 1, 1), last)
        col_out[e, 0] = first
        col_out[e, 1] = last
        copies.append(send(e, 2, col_out.at[e, 1], col_in.at[e, 0]))
        copies.append(send(e, 3, col_out.at[e, 0], col_in.at[e, 1]))
        for s in range(S):
            split_own(e, s)

        def finish():
            for c in copies:
                c.wait_recv()
            split_halo(e)

        return finish

    def start_change(e, change, fill):
        note_out[e // 2] = jnp.concatenate(
            [index_row.astype(f32), to_row(change), jnp.zeros((6, K), f32)], axis=0)
        copies = [send(e, i, note_out.at[e // 2], note_in.at[e // 2, i]) for i in range(4)]
        for s in range(S):
            fill(s)
            split_own(e, s)

        def finish():
            for c in copies:
                c.wait_recv()
            for i in range(4):
                there = note_in[e // 2, i]
                at_row = there[0:1].astype(jnp.int32)
                at = to_column(there[0:1]).astype(jnp.int32)
                by = to_column(there[1:2])
                if i < 2:
                    s, halo = ((S - 1, 0), (0, S + 1))[i]
                    hot = (iota((N, K), 0) + s * N == row_of(at_row)).astype(f32).astype(bf16)
                    vh, vl = split(jnp.where(iota((K, X), 1) == (at & (X - 1)), by, 0.0))
                    halo = slice(halo * N, (halo + 1) * N)
                    fields[e, halo, :] = fields[e - 2, halo, :] + (mm(hot, vh) + mm(hot, vl))
                else:
                    edge = (X - 1, 0)[i - 2]
                    node = at_row >> (shift_x + shift_s)
                    hot = (iota((N, K), 0) == node).astype(f32).astype(bf16)
                    by = jnp.where((at & (X - 1)) == edge, by, 0.0)
                    s_of = (at >> shift_x) & (S - 1)
                    vh, vl = split(jnp.where(iota((K, LANES), 1) == s_of, by, 0.0))
                    col_in[e, i - 2] = col_in[e - 2, i - 2] + (mm(hot, vh) + mm(hot, vl))
            split_halo(e)

        return finish

    def apply(e, target, finish):
        f, h, l = fields.at[e], high.at[e % 2], low.at[e % 2]

        def element_row(s):
            near = slice(s * N, (s + 3) * N)
            xh, xl = h[near, :], l[near, :]
            p = mm(big[...], xh)
            r = p[: 3 * N] + p[3 * N :] + mm(big[: 3 * N, :], xl)
            res = cs[s * N : (s + 1) * N, :] * f[own(s), :] + r[:N]
            res = res - jnp.where(wide == 0, 0.0, pltpu.roll(r[N : 2 * N], 1, 1))
            res = res - jnp.where(wide == X - 1, 0.0, pltpu.roll(r[2 * N :], X - 1, 1))
            target[own(s), :] = res

        for s in range(1, S - 1):
            element_row(s)
        finish()
        element_row(0)
        element_row(S - 1)
        edges = []
        for i, there in enumerate((xs > 0, xs < nxs - 1)):
            got = jnp.where(there, col_in[e, i], 0.0)
            gh, gl = split(got)
            edges.append(mm(side[i, 0], gh) + mm(side[i, 1], gh) + mm(side[i, 0], gl))

        def fill(s):
            first = pltpu.roll(edges[0], LANES - s, 1) if s else edges[0]
            target[own(s), :LANES] = target[own(s), :LANES] - jnp.where(lane == 0, first, 0.0)
            last = pltpu.roll(edges[1], LANES - 1 - s, 1)
            target[own(s), X - LANES :] = target[own(s), X - LANES :] - jnp.where(lane == LANES - 1, last, 0.0)

        return fill

    def traces(e):
        h, l = high.at[e % 2], low.at[e % 2]
        body = slice(N, (S + 1) * N)
        t = mm(pick_t[...], h[body, :]) + mm(pick_t[...], l[body, :])
        return to_row(jnp.sum(t * where_x[...], axis=1, keepdims=True))

    def fold(v):
        v = jnp.sum(v, axis=0, keepdims=True)
        return functools.reduce(lambda a, b: a + b, [v[:, i : i + LANES] for i in range(0, X, LANES)])

    def products(pairs):
        res = []
        for a, b in pairs:
            acc = None
            for s in range(S):
                t = a[own(s), :] * b[own(s), :]
                acc = t if acc is None else acc + t
            res.append(fold(acc))
        return res

    d = to_column(disp0[...])
    fetch[0].wait()
    for sub in range(SUBITERS):
        er, ew = 2 * sub, 2 * sub + 1
        r, w, u = fields.at[er], fields.at[ew], fields.at[2 * SUBITERS]
        dh, dl = split(d * where_x[...])
        push = jnp.concatenate([dh, dl], axis=0)

        def fill_rhs(s):
            mine = slice(s * N, (s + 1) * N)
            if sub == 0:
                hot = (iota((N, K), 0) + s * N == place).astype(f32).astype(bf16)
                pick[mine, :K] = hot
                pick[mine, K:] = hot
                base[mine, :] = src[:, s, :]
            r[own(s), :] = base[mine, :] + mm(pick[mine, :], push)

        finish = start_change(er, change, fill_rhs) if sub else start_halo(er, fill_rhs)
        if sub == 0:
            prepare()
        finish = start_halo(ew, apply(er, w, finish))
        rt, wt = traces(er), traces(ew)
        rr, rw, ww = products([(r, r), (r, w), (w, w)])
        fill = apply(ew, u, finish)
        for s in range(S):
            fill(s)
        ru, wu, uu = products([(r, u), (w, u), (u, u)])
        mine = jnp.concatenate([rt, wt, rr, rw, ru, ww, wu, uu], axis=0)
        part[sub] = mine
        copies = []
        for o in range(1, nxs):
            c = pltpu.make_async_remote_copy(
                src_ref=part.at[sub], dst_ref=part_in.at[sub, xs],
                send_sem=xs_send.at[sub, o], recv_sem=xs_recv.at[sub, o],
                device_id={"xs": lax.rem(xs + o, nxs)}, device_id_type=MESH)
            c.start()
            copies.append(c)
            sent.append(c)
        part_in[sub, xs] = mine
        for c in copies:
            c.wait_recv()
        acc = part_in[sub, 0]
        for i in range(1, nxs):
            acc = acc + part_in[sub, i]
        total[sub] = acc
        copies = []
        for o in range(1, nsp):
            c = pltpu.make_async_remote_copy(
                src_ref=total.at[sub], dst_ref=total_in.at[sub, sp],
                send_sem=sp_send.at[sub, o], recv_sem=sp_recv.at[sub, o],
                device_id={"span": lax.rem(sp + o, nsp)}, device_id_type=MESH)
            c.start()
            copies.append(c)
            sent.append(c)
        total_in[sub, sp] = acc
        if sub == 0:
            fetch[8].wait()
        y = []
        for j in range(2):
            a = jnp.zeros((comp.shape[0], K), f32)
            for i in range(nxs):
                a = a + comp[:, i * K : (i + 1) * K] * part_in[sub, i, j : j + 1, :]
            y.append(jnp.sum(a, axis=1, keepdims=True))
        for c in copies:
            c.wait_recv()
        acc = total_in[sub, 0]
        for i in range(1, nsp):
            acc = acc + total_in[sub, i]
        g = jnp.sum(acc, axis=1, keepdims=True)
        rr, rw, ru, ww, wu, uu = [g[i : i + 1, :] for i in range(2, 8)]
        c0 = SHIFT
        g11 = ww + 2.0 * c0 * rw + c0 * c0 * rr
        g12 = wu + c0 * (ww + ru) + c0 * c0 * rw
        g22 = uu + 2.0 * c0 * wu + c0 * c0 * ww
        b1 = rw + c0 * rr
        b2 = ru + c0 * rw
        det = g11 * g22 - g12 * g12
        ca = (b1 * g22 - b2 * g12) / det
        cb = (b2 * g11 - b1 * g12) / det
        change = 0.5 * (ca * y[0] + cb * y[1]) - 0.5 * d
        d = 0.5 * (ca * y[0] + cb * y[1]) + 0.5 * d
    for s in range(S):
        src[:, s, :] = ca * r[own(s), :] + cb * w[own(s), :]
    leaving = pltpu.make_async_copy(src, out, out_sem)
    leaving.start()
    dout[0] = to_row(d)
    for c in sent:
        c.wait_send()
    leaving.wait()


def body(nsp, nxs, source, coefficient, volume, slo, sup, clo, cup, interface, compliance, start):
    N, S, X = source.shape
    K = interface.shape[2]
    M = compliance.shape[1]
    E = 2 * SUBITERS
    vm = pl.BlockSpec(memory_space=pltpu.VMEM)
    hbm = pl.BlockSpec(memory_space=pltpu.HBM)
    tall = (S + 2) * N
    dma = pltpu.SemaphoreType.DMA
    args = (source, coefficient, volume, slo, sup, clo, cup,
            interface.reshape(1, K), compliance.reshape(M, compliance.shape[2]), start.reshape(1, K))
    out, disp = pl.pallas_call(
        functools.partial(window, (nsp, nxs, N, S, X, K)),
        out_shape=(jax.ShapeDtypeStruct((N, S, X), f32), jax.ShapeDtypeStruct((1, 1, K), f32)),
        in_specs=[hbm] * 10,
        out_specs=(hbm, vm),
        scratch_shapes=[pltpu.VMEM(a.shape, a.dtype) for a in args] + [
            pltpu.VMEM((6 * N, 3 * N), bf16),
            pltpu.VMEM((2, 2, N, N), bf16),
            pltpu.VMEM((S * N, X), f32),
            pltpu.VMEM((S * N, X), f32),
            pltpu.VMEM((E + 1, tall, X), f32),
            pltpu.VMEM((2, tall, X), bf16),
            pltpu.VMEM((2, tall, X), bf16),
            pltpu.VMEM((S * N, 2 * K), bf16),
            pltpu.VMEM((K, S * N), bf16),
            pltpu.VMEM((K, X), f32),
            pltpu.VMEM((E, 2, N, LANES), f32),
            pltpu.VMEM((E, 2, N, LANES), f32),
            pltpu.VMEM((SUBITERS, 8, LANES), f32),
            pltpu.VMEM((SUBITERS, nxs, 8, LANES), f32),
            pltpu.VMEM((SUBITERS, 8, LANES), f32),
            pltpu.VMEM((SUBITERS, nsp, 8, LANES), f32),
            dma((E, 4)), dma((E, 4)),
            dma((SUBITERS, nxs)), dma((SUBITERS, nxs)),
            dma((SUBITERS, nsp)), dma((SUBITERS, nsp)),
            pltpu.VMEM((SUBITERS, 8, K), f32),
            pltpu.VMEM((SUBITERS, 4, 8, K), f32),
            dma((10,)), dma,
        ],
        compiler_params=pltpu.CompilerParams(
            collective_id=0, has_side_effects=True, vmem_limit_bytes=64 * 1024 * 1024),
        cost_estimate=pl.CostEstimate(flops=2 ** 30, bytes_accessed=2 ** 21, transcendentals=0),
        name="coupling_window",
    )(*args)
    return out, disp


def solution(mesh):
    field, shell = P(None, "span", "xs"), P("span", "xs", None)
    return jax.shard_map(
        functools.partial(body, mesh.shape["span"], mesh.shape["xs"]),
        mesh=mesh,
        in_specs=(field, field, P(), P(), P(), P(), P(), shell, shell, shell),
        out_specs=(field, shell),
        check_vma=False,
    )
```

```python
import functools

import jax
import jax.numpy as jnp
from jax import lax
from jax.experimental import pallas as pl
from jax.experimental.pallas import tpu as pltpu
from jax.sharding import PartitionSpec as P

SUBITERS = 2
SHIFT = 3.75
LANES = 128
MESH = pl.DeviceIdType.MESH
f32, bf16 = jnp.float32, jnp.bfloat16


def split(value):
    high = value.astype(bf16)
    return high, (value - high.astype(f32)).astype(bf16)


def mm(a, b):
    return jnp.dot(a, b, preferred_element_type=f32)


def iota(shape, dim):
    return lax.broadcasted_iota(jnp.int32, shape, dim)


def to_column(row):
    k = row.shape[1]
    wide = jnp.broadcast_to(row, (k, k))
    keep = iota((k, k), 0) == iota((k, k), 1)
    return jnp.sum(jnp.where(keep, wide, jnp.zeros_like(wide)), axis=1, keepdims=True)


def to_row(column):
    k = column.shape[0]
    wide = jnp.broadcast_to(column, (k, k))
    keep = iota((k, k), 0) == iota((k, k), 1)
    return jnp.sum(jnp.where(keep, wide, jnp.zeros_like(wide)), axis=0, keepdims=True)


def window(dims, *refs):
    given, refs = refs[:10], refs[10:]
    out, dout, refs = refs[0], refs[1], refs[2:]
    held, refs = refs[:10], refs[10:]
    run_window(dims, given, held, out, dout, *refs)


def run_window(dims, given, held, out, dout, big, side, cs, base, fields, high, low, pick, pick_t, where_x,
           col_out, col_in, part, part_in, total, total_in,
           halo_send, halo_recv, xs_send, xs_recv, sp_send, sp_recv,
           note_out, note_in, in_sem, out_sem):
    src, coef, vol, slo, sup, clo, cup, face, comp, disp0 = held
    fetch = [pltpu.make_async_copy(a, b, in_sem.at[i]) for i, (a, b) in enumerate(zip(given, held))]
    for i in (0, 7, 9, 2, 3, 4, 5, 6, 1, 8):
        fetch[i].start()
    nsp, nxs, N, S, X, K = dims
    sp, xs = lax.axis_index("span"), lax.axis_index("xs")
    barrier = pltpu.get_barrier_semaphore()
    for o in range(1, nxs):
        pl.semaphore_signal(barrier, inc=1, device_id={"xs": lax.rem(xs + o, nxs)}, device_id_type=MESH)
    for o in range(1, nsp):
        pl.semaphore_signal(barrier, inc=1, device_id={"span": lax.rem(sp + o, nsp)}, device_id_type=MESH)

    fetch[7].wait()
    fetch[9].wait()

    index_row = face[...]
    index_col = to_column(index_row.astype(f32)).astype(jnp.int32)

    shift_x, shift_s = X.bit_length() - 1, S.bit_length() - 1

    def row_of(index):
        s = (index >> shift_x) & (S - 1)
        return s * N + (index >> (shift_x + shift_s))

    place = row_of(index_row)
    where_x[...] = (iota((K, X), 1) == (index_col & (X - 1))).astype(f32)

    def prepare():
        for i in range(2, 7):
            fetch[i].wait()
        zero = jnp.zeros((N, N), f32)
        rows = jnp.concatenate([
            jnp.concatenate([-slo[...], vol[...], -sup[...]], axis=1),
            jnp.concatenate([zero, clo[...], zero], axis=1),
            jnp.concatenate([zero, cup[...], zero], axis=1),
        ], axis=0)
        bh, bl = split(rows)
        big[: 3 * N, :] = bh
        big[3 * N :, :] = bl
        for i, m in enumerate((clo, cup)):
            mh, ml = split(m[...])
            side[i, 0] = mh
            side[i, 1] = ml
        pick_t[...] = (iota((K, S * N), 1) == row_of(index_col)).astype(f32).astype(bf16)
        fetch[1].wait()
        for s in range(S):
            cs[s * N : (s + 1) * N, :] = coef[:, s, :] - SHIFT

    lane = iota((N, LANES), 1)
    wide = iota((N, X), 1)
    sent = []

    def own(s):
        return slice((s + 1) * N, (s + 2) * N)

    up, down = lax.rem(sp + 1, nsp), lax.rem(sp + nsp - 1, nsp)
    right, left = lax.rem(xs + 1, nxs), lax.rem(xs + nxs - 1, nxs)
    towards = (("span", up), ("span", down), ("xs", right), ("xs", left))
    order = [0, S - 1] + list(range(1, S - 1))

    def send(e, i, from_ref, to_ref):
        axis, target = towards[i]
        c = pltpu.make_async_remote_copy(
            src_ref=from_ref, dst_ref=to_ref, send_sem=halo_send.at[e, i], recv_sem=halo_recv.at[e, i],
            device_id={axis: target}, device_id_type=MESH)
        c.start()
        sent.append(c)
        return c

    def split_own(e, s):
        high[e % 2, own(s), :], low[e % 2, own(s), :] = split(fields[e, own(s), :])

    def split_halo(e):
        for row in (slice(0, N), slice((S + 1) * N, (S + 2) * N)):
            high[e % 2, row, :], low[e % 2, row, :] = split(fields[e, row, :])

    def start_halo(e, fill):
        f = fields.at[e]
        fill(0)
        fill(S - 1)
        if e == 0:
            pl.semaphore_wait(barrier, nxs + nsp - 2)
        copies = [
            send(e, 0, f.at[pl.ds(S * N, N)], f.at[pl.ds(0, N)]),
            send(e, 1, f.at[pl.ds(N, N)], f.at[pl.ds((S + 1) * N, N)]),
        ]
        first = jnp.zeros((N, LANES), f32)
        last = jnp.zeros((N, LANES), f32)
        for s in order:
            if 0 < s < S - 1:
                fill(s)
            a = f[own(s), :LANES]
            b = f[own(s), X - LANES :]
            first = jnp.where(lane == s, pltpu.roll(a, s, 1) if s else a, first)
            last = jnp.where(lane == s, pltpu.roll(b, s + 1, 1), last)
        col_out[e, 0] = first
        col_out[e, 1] = last
        copies.append(send(e, 2, col_out.at[e, 1], col_in.at[e, 0]))
        copies.append(send(e, 3, col_out.at[e, 0], col_in.at[e, 1]))
        for s in range(S):
            split_own(e, s)

        def finish():
            for c in copies:
                c.wait_recv()
            split_halo(e)

        return finish

    def start_change(e, change, fill):
        note_out[e // 2] = jnp.concatenate(
            [index_row.astype(f32), to_row(change), jnp.zeros((6, K), f32)], axis=0)
        copies = [send(e, i, note_out.at[e // 2], note_in.at[e // 2, i]) for i in range(4)]
        for s in range(S):
            fill(s)
            split_own(e, s)

        def finish():
            for i in (2, 3, 0, 1):
                copies[i].wait_recv()
                there = note_in[e // 2, i]
                at_row = there[0:1].astype(jnp.int32)
                at = to_column(there[0:1]).astype(jnp.int32)
                by = to_column(there[1:2])
                if i < 2:
                    s, halo = ((S - 1, 0), (0, S + 1))[i]
                    hot = (iota((N, K), 0) + s * N == row_of(at_row)).astype(f32).astype(bf16)
                    vh, vl = split(jnp.where(iota((K, X), 1) == (at & (X - 1)), by, 0.0))
                    halo = slice(halo * N, (halo + 1) * N)
                    fields[e, halo, :] = fields[e - 2, halo, :] + (mm(hot, vh) + mm(hot, vl))
                else:
                    edge = (X - 1, 0)[i - 2]
                    node = at_row >> (shift_x + shift_s)
                    hot = (iota((N, K), 0) == node).astype(f32).astype(bf16)
                    by = jnp.where((at & (X - 1)) == edge, by, 0.0)
                    s_of = (at >> shift_x) & (S - 1)
                    vh, vl = split(jnp.where(iota((K, LANES), 1) == s_of, by, 0.0))
                    col_in[e, i - 2] = col_in[e - 2, i - 2] + (mm(hot, vh) + mm(hot, vl))
            split_halo(e)

        return finish

    def apply(e, target, finish):
        f, h, l = fields.at[e], high.at[e % 2], low.at[e % 2]

        def element_row(s):
            near = slice(s * N, (s + 3) * N)
            xh, xl = h[near, :], l[near, :]
            p = mm(big[...], xh)
            r = p[: 3 * N] + p[3 * N :] + mm(big[: 3 * N, :], xl)
            res = cs[s * N : (s + 1) * N, :] * f[own(s), :] + r[:N]
            res = res - jnp.where(wide == 0, 0.0, pltpu.roll(r[N : 2 * N], 1, 1))
            res = res - jnp.where(wide == X - 1, 0.0, pltpu.roll(r[2 * N :], X - 1, 1))
            target[own(s), :] = res

        for s in range(1, S - 1):
            element_row(s)
        finish()
        element_row(0)
        element_row(S - 1)
        edges = []
        for i, there in enumerate((xs > 0, xs < nxs - 1)):
            got = jnp.where(there, col_in[e, i], 0.0)
            gh, gl = split(got)
            edges.append(mm(side[i, 0], gh) + mm(side[i, 1], gh) + mm(side[i, 0], gl))

        def fill(s):
            first = pltpu.roll(edges[0], LANES - s, 1) if s else edges[0]
            target[own(s), :LANES] = target[own(s), :LANES] - jnp.where(lane == 0, first, 0.0)
            last = pltpu.roll(edges[1], LANES - 1 - s, 1)
            target[own(s), X - LANES :] = target[own(s), X - LANES :] - jnp.where(lane == LANES - 1, last, 0.0)

        return fill

    def traces(e):
        h, l = high.at[e % 2], low.at[e % 2]
        body = slice(N, (S + 1) * N)
        t = mm(pick_t[...], h[body, :]) + mm(pick_t[...], l[body, :])
        return to_row(jnp.sum(t * where_x[...], axis=1, keepdims=True))

    def fold(v):
        v = jnp.sum(v, axis=0, keepdims=True)
        return functools.reduce(lambda a, b: a + b, [v[:, i : i + LANES] for i in range(0, X, LANES)])

    def products(pairs):
        res = []
        for a, b in pairs:
            acc = None
            for s in range(S):
                t = a[own(s), :] * b[own(s), :]
                acc = t if acc is None else acc + t
            res.append(fold(acc))
        return res

    d = to_column(disp0[...])
    fetch[0].wait()
    for sub in range(SUBITERS):
        er, ew = 2 * sub, 2 * sub + 1
        r, w, u = fields.at[er], fields.at[ew], fields.at[2 * SUBITERS]
        dh, dl = split(d * where_x[...])
        push = jnp.concatenate([dh, dl], axis=0)

        def fill_rhs(s):
            mine = slice(s * N, (s + 1) * N)
            if sub == 0:
                hot = (iota((N, K), 0) + s * N == place).astype(f32).astype(bf16)
                pick[mine, :K] = hot
                pick[mine, K:] = hot
                base[mine, :] = src[:, s, :]
            r[own(s), :] = base[mine, :] + mm(pick[mine, :], push)

        finish = start_change(er, change, fill_rhs) if sub else start_halo(er, fill_rhs)
        if sub == 0:
            prepare()
        finish = start_halo(ew, apply(er, w, finish))
        rt, wt = traces(er), traces(ew)
        rr, rw, ww = products([(r, r), (r, w), (w, w)])
        fill = apply(ew, u, finish)
        for s in range(S):
            fill(s)
        ru, wu, uu = products([(r, u), (w, u), (u, u)])
        mine = jnp.concatenate([rt, wt, rr, rw, ru, ww, wu, uu], axis=0)
        part[sub] = mine
        copies = []
        for o in range(1, nxs):
            c = pltpu.make_async_remote_copy(
                src_ref=part.at[sub], dst_ref=part_in.at[sub, xs],
                send_sem=xs_send.at[sub, o], recv_sem=xs_recv.at[sub, o],
                device_id={"xs": lax.rem(xs + o, nxs)}, device_id_type=MESH)
            c.start()
            copies.append(c)
            sent.append(c)
        part_in[sub, xs] = mine
        for c in copies:
            c.wait_recv()
        acc = part_in[sub, 0]
        for i in range(1, nxs):
            acc = acc + part_in[sub, i]
        total[sub] = acc
        copies = []
        for o in range(1, nsp):
            c = pltpu.make_async_remote_copy(
                src_ref=total.at[sub], dst_ref=total_in.at[sub, sp],
                send_sem=sp_send.at[sub, o], recv_sem=sp_recv.at[sub, o],
                device_id={"span": lax.rem(sp + o, nsp)}, device_id_type=MESH)
            c.start()
            copies.append(c)
            sent.append(c)
        total_in[sub, sp] = acc
        if sub == 0:
            fetch[8].wait()
        y = []
        for j in range(2):
            a = jnp.zeros((comp.shape[0], K), f32)
            for i in range(nxs):
                a = a + comp[:, i * K : (i + 1) * K] * part_in[sub, i, j : j + 1, :]
            y.append(jnp.sum(a, axis=1, keepdims=True))
        for c in copies:
            c.wait_recv()
        acc = total_in[sub, 0]
        for i in range(1, nsp):
            acc = acc + total_in[sub, i]
        g = jnp.sum(acc, axis=1, keepdims=True)
        rr, rw, ru, ww, wu, uu = [g[i : i + 1, :] for i in range(2, 8)]
        c0 = SHIFT
        g11 = ww + 2.0 * c0 * rw + c0 * c0 * rr
        g12 = wu + c0 * (ww + ru) + c0 * c0 * rw
        g22 = uu + 2.0 * c0 * wu + c0 * c0 * ww
        b1 = rw + c0 * rr
        b2 = ru + c0 * rw
        det = g11 * g22 - g12 * g12
        ca = (b1 * g22 - b2 * g12) / det
        cb = (b2 * g11 - b1 * g12) / det
        change = 0.5 * (ca * y[0] + cb * y[1]) - 0.5 * d
        d = 0.5 * (ca * y[0] + cb * y[1]) + 0.5 * d
    for s in range(S):
        src[:, s, :] = ca * r[own(s), :] + cb * w[own(s), :]
    leaving = pltpu.make_async_copy(src, out, out_sem)
    leaving.start()
    dout[0] = to_row(d)
    for c in sent:
        c.wait_send()
    leaving.wait()


def body(nsp, nxs, source, coefficient, volume, slo, sup, clo, cup, interface, compliance, start):
    N, S, X = source.shape
    K = interface.shape[2]
    M = compliance.shape[1]
    E = 2 * SUBITERS
    vm = pl.BlockSpec(memory_space=pltpu.VMEM)
    hbm = pl.BlockSpec(memory_space=pltpu.HBM)
    tall = (S + 2) * N
    dma = pltpu.SemaphoreType.DMA
    args = (source, coefficient, volume, slo, sup, clo, cup,
            interface.reshape(1, K), compliance.reshape(M, compliance.shape[2]), start.reshape(1, K))
    out, disp = pl.pallas_call(
        functools.partial(window, (nsp, nxs, N, S, X, K)),
        out_shape=(jax.ShapeDtypeStruct((N, S, X), f32), jax.ShapeDtypeStruct((1, 1, K), f32)),
        in_specs=[hbm] * 10,
        out_specs=(hbm, vm),
        scratch_shapes=[pltpu.VMEM(a.shape, a.dtype) for a in args] + [
            pltpu.VMEM((6 * N, 3 * N), bf16),
            pltpu.VMEM((2, 2, N, N), bf16),
            pltpu.VMEM((S * N, X), f32),
            pltpu.VMEM((S * N, X), f32),
            pltpu.VMEM((E + 1, tall, X), f32),
            pltpu.VMEM((2, tall, X), bf16),
            pltpu.VMEM((2, tall, X), bf16),
            pltpu.VMEM((S * N, 2 * K), bf16),
            pltpu.VMEM((K, S * N), bf16),
            pltpu.VMEM((K, X), f32),
            pltpu.VMEM((E, 2, N, LANES), f32),
            pltpu.VMEM((E, 2, N, LANES), f32),
            pltpu.VMEM((SUBITERS, 8, LANES), f32),
            pltpu.VMEM((SUBITERS, nxs, 8, LANES), f32),
            pltpu.VMEM((SUBITERS, 8, LANES), f32),
            pltpu.VMEM((SUBITERS, nsp, 8, LANES), f32),
            dma((E, 4)), dma((E, 4)),
            dma((SUBITERS, nxs)), dma((SUBITERS, nxs)),
            dma((SUBITERS, nsp)), dma((SUBITERS, nsp)),
            pltpu.VMEM((SUBITERS, 8, K), f32),
            pltpu.VMEM((SUBITERS, 4, 8, K), f32),
            dma((10,)), dma,
        ],
        compiler_params=pltpu.CompilerParams(
            collective_id=0, has_side_effects=True, vmem_limit_bytes=64 * 1024 * 1024),
        cost_estimate=pl.CostEstimate(flops=2 ** 30, bytes_accessed=2 ** 21, transcendentals=0),
        name="coupling_window",
    )(*args)
    return out, disp


def solution(mesh):
    field, shell = P(None, "span", "xs"), P("span", "xs", None)
    return jax.shard_map(
        functools.partial(body, mesh.shape["span"], mesh.shape["xs"]),
        mesh=mesh,
        in_specs=(field, field, P(), P(), P(), P(), P(), shell, shell, shell),
        out_specs=(field, shell),
        check_vma=False,
    )
```
